256 devices in a mesh: tm: 16 (over x, z_hi, core), track: 16 (over z_lo, y).
Axes of the slice: x: 4, y: 4, z: 8 (z_hi: 2, z_lo: 4; z = z_hi * 4 + z_lo), core: 2. Of those that a mesh axis runs over, the one named last changes fastest.
Arguments:
- query_rows: bfloat16 [1024, 2, 16, 1024], P('tm', None, 'track'), may hold values from -10 to 10
- key_rows: bfloat16 [1024, 2, 16, 1024], P('tm', None, 'track'), may hold values from -10 to 10
- value_rows: bfloat16 [1024, 2, 16, 1024], P('tm', None, 'track'), may hold values from -6 to 6
- grad_output: bfloat16 [1024, 2, 16, 1024], P('tm', None, 'track'), may hold values from -6 to 6
- out_weight: bfloat16 [1024, 1024], P(None, 'track'), may hold values from -0.1875 to 0.1875
Outputs:
- grad_query: bfloat16 [1024, 2, 16, 1024], P('tm', None, 'track')
- grad_key: bfloat16 [1024, 2, 16, 1024], P('tm', None, 'track')
- grad_value: bfloat16 [1024, 2, 16, 1024], P('tm', None, 'track')
- grad_weight: float32 [1024, 1024], P(('tm', 'track'))
The draws below stay inside these ranges and needn't reach their ends.
All inputs are finite; a program needn't handle non-finite values.
Results may differ from the reference program's by a relative error of at most 0.012.
Values may be sent and summed in bfloat16 or wider, within the bound.
No kernel may reach another device: no remote copies, remote signals or barrier semaphores. Data moves between devices by JAX's collectives and lax.ppermute only.
A program may use at most 128 MiB of HBM per device.

```python
import math
import jax
import jax.numpy as jnp
from jax import lax

D = 1024
HEADS = 8
HEAD = 128
STEPS_DEV = 64
SCORES = 2
STEPS = 1024
TRACKS = 16
N_TM = 16


def draw_query_rows(key, part):
    key = jax.random.fold_in(key, 1)
    complete_shape = (STEPS, SCORES, TRACKS, D)
    drawn = 1.2 * jax.random.truncated_normal(key, -5.0, 5.0, complete_shape, jnp.float32)
    return drawn.astype(jnp.bfloat16)


def draw_key_rows(key, part):
    key = jax.random.fold_in(key, 2)
    complete_shape = (STEPS, SCORES, TRACKS, D)
    drawn = 1.2 * jax.random.truncated_normal(key, -5.0, 5.0, complete_shape, jnp.float32)
    return drawn.astype(jnp.bfloat16)


def levels(own_key, dims, shards, smallest, largest):
    def one(position, blocks):
        steps = jax.random.uniform(jax.random.fold_in(jax.random.fold_in(own_key, 6), position), (blocks,), jnp.float32, smallest / len(shards), largest / len(shards))
        return jnp.repeat(jnp.exp(steps), dims[position] // blocks).reshape((-1,) + (1,) * (len(dims) - position - 1))

    gain = one(*shards[0])
    for cut in shards[1:]:
        gain = gain * one(*cut)
    return gain


def gaussian(key, extent, deviation, most, split=(), kind=jnp.bfloat16):
    values = deviation * jax.random.normal(key, extent, jnp.float32)
    if split:
        values = values * levels(key, extent, split, -0.22, 0.18)
    return jnp.clip(values, -most, most).astype(kind)


def setup_inputs(seed: int = 0) -> dict:
    key_list = jax.random.split(jax.random.key(seed), 6)
    return {
        "query_rows": draw_query_rows(jax.random.fold_in(key_list[5], 71), 0),
        "key_rows": draw_key_rows(jax.random.fold_in(key_list[5], 71), 0),
        "value_rows": gaussian(key_list[2], (STEPS, SCORES, TRACKS, D), 1.0, 6.0, ((0, 16), (2, 16))),
        "grad_output": gaussian(key_list[3], (STEPS, SCORES, TRACKS, D), 1.0, 6.0, ((0, 16), (2, 16))),
        "out_weight": gaussian(key_list[4], (D, D), D ** -0.5, 0.1875, ((1, 16),)),
    }


def attend_item(packed):
    item_query, item_key, item_value, item_grad = packed
    score_scale = HEAD ** (-0.5)
    logits = jnp.dot(item_query, item_key.T, preferred_element_type=jnp.float32) * score_scale
    places = jnp.arange(STEPS)
    visible = places[None, :] <= places[:, None]
    logits = jnp.where(visible, logits, -1e+30)
    row_peak = lax.optimization_barrier(jnp.max(logits, axis=1, keepdims=True))
    weights = jnp.exp(logits - row_peak)
    probs_full = weights / lax.optimization_barrier(jnp.sum(weights, axis=1, keepdims=True))
    probs_low = probs_full.astype(jnp.bfloat16)
    attended = jnp.dot(probs_low, item_value, preferred_element_type=jnp.float32).astype(jnp.bfloat16)
    dprobs = jnp.dot(item_grad, item_value.T, preferred_element_type=jnp.float32)
    row_delta = lax.optimization_barrier(jnp.sum(probs_full * dprobs, axis=1, keepdims=True))
    dscores = (probs_full * (dprobs - row_delta) * score_scale).astype(jnp.bfloat16)
    grad_query = jnp.dot(dscores, item_key, preferred_element_type=jnp.float32).astype(jnp.bfloat16)
    score_grad_blocks = dscores.reshape(N_TM, STEPS_DEV, STEPS).astype(jnp.float32)
    probability_blocks = probs_low.reshape(N_TM, STEPS_DEV, STEPS).astype(jnp.float32)
    query_row_blocks = item_query.reshape(N_TM, STEPS_DEV, HEAD).astype(jnp.float32)
    output_grad_blocks = item_grad.reshape(N_TM, STEPS_DEV, HEAD).astype(jnp.float32)
    key_grad_pieces = jnp.einsum('vur,vuj->vrj', score_grad_blocks, query_row_blocks)
    value_grad_pieces = jnp.einsum('vur,vuj->vrj', probability_blocks, output_grad_blocks)
    key_grad_pieces = lax.optimization_barrier(key_grad_pieces.astype(jnp.bfloat16)).astype(jnp.float32)
    value_grad_pieces = lax.optimization_barrier(value_grad_pieces.astype(jnp.bfloat16)).astype(jnp.float32)
    grad_key = lax.optimization_barrier(jnp.sum(key_grad_pieces, axis=0)).astype(jnp.bfloat16)
    grad_value = lax.optimization_barrier(jnp.sum(value_grad_pieces, axis=0)).astype(jnp.bfloat16)
    return (attended, grad_query, grad_key, grad_value)

def reference(query_rows, key_rows, value_rows, grad_output, out_weight):
    flat_grad = grad_output.reshape(STEPS * SCORES * TRACKS, D)
    attn_grad = jnp.dot(flat_grad, out_weight.T, preferred_element_type=jnp.float32).astype(jnp.bfloat16)
    attn_grad = attn_grad.reshape(STEPS, SCORES, TRACKS, D)

    def to_items(array):
        return array.reshape(STEPS, SCORES * TRACKS * HEADS, HEAD).transpose(1, 0, 2)

    def from_items(array):
        return array.transpose(1, 0, 2).reshape(STEPS, SCORES, TRACKS, D)
    results = lax.map(attend_item, (to_items(query_rows), to_items(key_rows), to_items(value_rows), to_items(attn_grad)))
    attended, grad_query, grad_key, grad_value = [from_items(item) for item in results]
    norm_factor = 1.0 / math.sqrt(STEPS * SCORES * TRACKS)
    grad_weight = jnp.dot(attended.reshape(STEPS * SCORES * TRACKS, D).T, flat_grad, preferred_element_type=jnp.float32) * norm_factor
    return (grad_query, grad_key, grad_value, grad_weight)
```

```python
import functools
import math

import jax
import jax.numpy as jnp
from jax import lax
from jax.experimental import pallas as pl
from jax.experimental.pallas import tpu as pltpu
from jax.sharding import PartitionSpec as P

HEADS = 8
HEAD = 128
BLOCK = 64
ROWS = 256


def dot(a, b, ca, cb):
    return lax.dot_general(
        a, b, (((ca,), (cb,)), ((), ())), preferred_element_type=jnp.float32
    )


def attention_kernel(
    n_tm, norm_factor, where_ref, qkv_ref, *refs
):
    piece_refs, weight_refs = refs[:8], refs[8:13]
    grads_ref, keep_ref, send_ref = refs[13:16]
    w_ref, do_ref, att_ref, gk_ref, gv_ref, gw_ref = refs[16:]
    length = n_tm * BLOCK
    x, z, core, track = where_ref[0], where_ref[1], where_ref[2], where_ref[3]

    chunk = w_ref.shape[0] // 16
    position = 0
    for ref in weight_refs:
        for j in range(ref.shape[0] // chunk):
            reverse = int(format(position, "04b")[::-1], 2)
            owner = track ^ reverse
            w_ref[pl.ds(pl.multiple_of(owner * chunk, chunk), chunk), :] = ref[
                j * chunk : (j + 1) * chunk, :
            ]
            position += 1

    def block_rows(piece, sub):
        dz, d = piece // 4, piece % 4
        block = 4 * ((x + 4 - d) % 4) + 2 * (z ^ dz) + (core ^ sub)
        return pl.ds(pl.multiple_of(block * BLOCK, BLOCK), BLOCK)

    for piece in range(8):
        part = dot(piece_refs[piece][...], w_ref[...], 1, 0).astype(jnp.bfloat16)
        do_ref[block_rows(piece, 0), :] = part[:BLOCK]
        do_ref[block_rows(piece, 1), :] = part[BLOCK:]

    scale = HEAD ** (-0.5)
    steps = ROWS // BLOCK
    for i in range(length // ROWS):
        width = (i + 1) * ROWS
        rows = slice(i * ROWS, (i + 1) * ROWS)
        blocks = slice(i * steps, (i + 1) * steps)
        q = qkv_ref[blocks, 0].reshape(ROWS, HEAD)
        k = qkv_ref[: (i + 1) * steps, 1].reshape(width, HEAD)
        v = qkv_ref[: (i + 1) * steps, 2].reshape(width, HEAD)
        do = do_ref[rows, :]
        s = dot(q, k, 1, 1) * scale
        row_at = lax.broadcasted_iota(jnp.int32, s.shape, 0) + i * ROWS
        col_at = lax.broadcasted_iota(jnp.int32, s.shape, 1)
        s = jnp.where(col_at <= row_at, s, -1e30)
        peak = jnp.max(s, axis=1, keepdims=True)
        e = jnp.exp(s - peak)
        p = e / jnp.sum(e, axis=1, keepdims=True)
        p_low = p.astype(jnp.bfloat16)
        att_ref[rows, :] = dot(p_low, v, 1, 0).astype(jnp.bfloat16)
        dp = dot(do, v, 1, 1)
        delta = jnp.sum(p * dp, axis=1, keepdims=True)
        ds = (p * (dp - delta) * scale).astype(jnp.bfloat16)
        gq = dot(ds, k, 1, 0).astype(jnp.bfloat16)
        grads_ref[blocks, 0] = gq.reshape(steps, BLOCK, HEAD)
        gk = dot(q, ds, 0, 0)
        gv = dot(do, p_low, 0, 0)
        if i:
            gk_ref[:, : width - ROWS] += gk[:, : width - ROWS]
            gv_ref[:, : width - ROWS] += gv[:, : width - ROWS]
            gk, gv = gk[:, width - ROWS :], gv[:, width - ROWS :]
        gk_ref[:, rows] = gk
        gv_ref[:, rows] = gv
    grads_ref[:, 1] = gk_ref[...].T.astype(jnp.bfloat16).reshape(n_tm, BLOCK, HEAD)
    grads_ref[:, 2] = gv_ref[...].T.astype(jnp.bfloat16).reshape(n_tm, BLOCK, HEAD)

    for piece in range(8):
        att = jnp.concatenate(
            [att_ref[block_rows(piece, 0), :], att_ref[block_rows(piece, 1), :]], axis=0
        )
        term = dot(att, piece_refs[piece][...], 0, 0)
        if piece == 0:
            gw_ref[...] = term
        else:
            gw_ref[...] += term
    half = HEAD // 2
    keep_ref[...] = gw_ref[pl.ds(pl.multiple_of(core * half, half), half), :] * norm_factor
    send_ref[...] = gw_ref[pl.ds(pl.multiple_of((1 - core) * half, half), half), :] * norm_factor


def attention(where, qkv, pieces, weights, n_tm, norm_factor):
    width = pieces[0].shape[1]
    length = n_tm * BLOCK
    vmem = pl.BlockSpec(memory_space=pltpu.VMEM)
    return pl.pallas_call(
        functools.partial(attention_kernel, n_tm, norm_factor),
        out_shape=(
            jax.ShapeDtypeStruct((n_tm, 3, BLOCK, HEAD), jnp.bfloat16),
            jax.ShapeDtypeStruct((HEAD // 2, width), jnp.float32),
            jax.ShapeDtypeStruct((HEAD // 2, width), jnp.float32),
        ),
        in_specs=[pl.BlockSpec(memory_space=pltpu.SMEM)] + [vmem] * (1 + len(pieces) + len(weights)),
        out_specs=(vmem, vmem, vmem),
        scratch_shapes=[
            pltpu.VMEM((width, HEAD), jnp.bfloat16),
            pltpu.VMEM((length, HEAD), jnp.bfloat16),
            pltpu.VMEM((length, HEAD), jnp.bfloat16),
            pltpu.VMEM((HEAD, length), jnp.float32),
            pltpu.VMEM((HEAD, length), jnp.float32),
            pltpu.VMEM((HEAD, width), jnp.float32),
        ],
        compiler_params=pltpu.CompilerParams(vmem_limit_bytes=48 * 1024 * 1024),
        cost_estimate=pl.CostEstimate(
            flops=2 * 6 * length * length * HEAD, bytes_accessed=4 << 20, transcendentals=length * length
        ),
        name="attention_backward",
    )(where, qkv, *pieces, *weights)


def swap(array, axis, mask):
    return lax.ppermute(array, axis, [(i, i ^ mask) for i in range(16)])


def local(query_rows, key_rows, value_rows, grad_output, out_weight):
    step_rows, score_count, track_local, model_width = query_rows.shape
    n_tm = lax.axis_size("tm")
    total_tokens = step_rows * n_tm * score_count * track_local * lax.axis_size("track")
    norm_factor = 1.0 / math.sqrt(total_tokens)
    tm = lax.axis_index("tm")
    track = lax.axis_index("track")
    x, z, core = tm // 4, (tm // 2) % 2, tm % 2
    head = tm // 2

    grads = grad_output.reshape(step_rows, score_count, model_width)
    first, second = grads[:, 0], grads[:, 1]
    mine = jnp.where(core == 0, first, second)
    other = jnp.where(core == 0, second, first)
    chip_piece = jnp.concatenate([mine, swap(other, "tm", 1)], axis=0)
    pieces = []
    for piece in (chip_piece, swap(chip_piece, "tm", 2)):
        pieces.append(piece)
        for d in (1, 2, 3):
            pieces.append(lax.ppermute(piece, "tm", [(i, (i + 4 * d) % 16) for i in range(16)]))

    held = lax.dynamic_slice_in_dim(out_weight.T, head * HEAD, HEAD, axis=1)
    weights = [held]
    for mask in (8, 4, 2, 1):
        got = swap(held, "track", mask)
        weights.append(got)
        held = jnp.concatenate([held, got], axis=0)

    qkv = jnp.stack([query_rows, key_rows, value_rows]).reshape(
        3, step_rows, score_count, HEADS, HEAD
    )
    qkv = qkv.transpose(3, 2, 0, 1, 4).reshape(n_tm, 3, step_rows, HEAD)
    qkv = lax.all_to_all(qkv, "tm", split_axis=0, concat_axis=0, tiled=True)

    where = jnp.stack([x, z, core, track]).astype(jnp.int32)
    item_grads, keep, send = attention(where, qkv, pieces, weights, n_tm, norm_factor)

    total = keep + swap(send, "tm", 1)
    total = total.reshape(2, 2, 2, 2, 4, model_width)
    for axis, mask in ((3, 1), (2, 2), (1, 4), (0, 8)):
        bit = (track & mask) != 0
        low = lax.index_in_dim(total, 0, axis, keepdims=True)
        high = lax.index_in_dim(total, 1, axis, keepdims=True)
        got = swap(jnp.where(bit, low, high), "track", mask)
        total = jnp.where(bit, high, low) + got
    grad_weight = total.reshape(4, model_width)

    returned = lax.all_to_all(item_grads, "tm", split_axis=0, concat_axis=0, tiled=True)
    returned = returned.reshape(HEADS, score_count, 3, step_rows, HEAD).transpose(2, 3, 1, 0, 4)
    returned = returned.reshape(3, step_rows, score_count, track_local, model_width)
    return (returned[0], returned[1], returned[2], grad_weight)


def solution(mesh):
    return jax.shard_map(
        local,
        mesh=mesh,
        in_specs=(
            P("tm", None, "track", None),
            P("tm", None, "track", None),
            P("tm", None, "track", None),
            P("tm", None, "track", None),
            P(None, "track"),
        ),
        out_specs=(
            P("tm", None, "track", None),
            P("tm", None, "track", None),
            P("tm", None, "track", None),
            P(("tm", "track"), None),
        ),
        check_vma=False,
    )
```

```python
import functools
import math

import jax
import jax.numpy as jnp
from jax import lax
from jax.experimental import pallas as pl
from jax.experimental.pallas import tpu as pltpu
from jax.sharding import PartitionSpec as P

HEADS = 8
HEAD = 128
BLOCK = 64
ROWS = 256


def dot(a, b, ca, cb):
    return lax.dot_general(
        a, b, (((ca,), (cb,)), ((), ())), preferred_element_type=jnp.float32
    )


def logits_of(qkv_ref, i):
    steps = ROWS // BLOCK
    width = (i + 1) * ROWS
    q = qkv_ref[i * steps : (i + 1) * steps, 0].reshape(ROWS, HEAD)
    k = qkv_ref[: (i + 1) * steps, 1].reshape(width, HEAD)
    v = qkv_ref[: (i + 1) * steps, 2].reshape(width, HEAD)
    s = dot(q, k, 1, 1) * (HEAD ** (-0.5) * math.log2(math.e))
    row_at = lax.broadcasted_iota(jnp.int32, s.shape, 0) + i * ROWS
    col_at = lax.broadcasted_iota(jnp.int32, s.shape, 1)
    return jnp.where(col_at <= row_at, s, -1e30), q, k, v


def forward_kernel(qkv_ref, att_ref, lse_ref):
    for i in range(att_ref.shape[0] // ROWS):
        rows = slice(i * ROWS, (i + 1) * ROWS)
        s, _, _, v = logits_of(qkv_ref, i)
        peak = jnp.max(s, axis=1, keepdims=True)
        e = jnp.exp2(s - peak)
        total = jnp.sum(e, axis=1, keepdims=True)
        p_low = (e * (1.0 / total)).astype(jnp.bfloat16)
        att_ref[rows, :] = dot(p_low, v, 1, 0).astype(jnp.bfloat16)
        lse_ref[rows, :] = peak + jnp.log2(total)


def chunks(places, piece_refs):
    tm = lax.axis_index("tm")
    x, z, core = tm // 4, (tm // 2) % 2, tm % 2
    for (far, back), ref in zip(places, piece_refs):
        for at in range(ref.shape[0] // (2 * BLOCK)):
            chip_x = at if back is None else (x + 4 - back) % 4
            first = 4 * chip_x + 2 * (z ^ far)
            rows = [
                pl.ds(pl.multiple_of((first + (core ^ sub)) * BLOCK, BLOCK), BLOCK) for sub in range(2)
            ]
            yield ref[at * 2 * BLOCK : (at + 1) * 2 * BLOCK, :], rows


def weight_kernel(norm_factor, places, att_ref, *refs):
    keep_ref, send_ref, gw_ref = refs[len(places) :]
    core = lax.axis_index("tm") % 2
    for n, (chunk, rows) in enumerate(chunks(places, refs)):
        att = jnp.concatenate([att_ref[r, :] for r in rows], axis=0)
        term = dot(att, chunk, 0, 0)
        if n == 0:
            gw_ref[...] = term
        else:
            gw_ref[...] += term
    half = HEAD // 2
    keep_ref[...] = gw_ref[pl.ds(pl.multiple_of(core * half, half), half), :] * norm_factor
    send_ref[...] = gw_ref[pl.ds(pl.multiple_of((1 - core) * half, half), half), :] * norm_factor


def backward_kernel(places, qkv_ref, lse_ref, *refs):
    weight_refs = refs[len(places) : len(places) + 4]
    grads_ref, w_ref, do_ref, gk_ref, gv_ref = refs[len(places) + 4 :]
    n_tm = qkv_ref.shape[0]
    length = n_tm * BLOCK

    track = lax.axis_index("track")
    size = w_ref.shape[0] // 16
    for p in range(16):
        owner = track ^ ((p % 4) * 4 + p // 4)
        w_ref[pl.ds(pl.multiple_of(owner * size, size), size), :] = weight_refs[p // 4][
            (p % 4) * size : (p % 4 + 1) * size, :
        ]
    for chunk, rows in chunks(places, refs):
        part = dot(chunk, w_ref[...], 1, 0).astype(jnp.bfloat16)
        do_ref[rows[0], :] = part[:BLOCK]
        do_ref[rows[1], :] = part[BLOCK:]

    scale = HEAD ** (-0.5)
    steps = ROWS // BLOCK
    for i in range(length // ROWS):
        width = (i + 1) * ROWS
        rows = slice(i * ROWS, (i + 1) * ROWS)
        do = do_ref[rows, :]
        s, q, k, v = logits_of(qkv_ref, i)
        p = jnp.exp2(s - lse_ref[rows, :])
        dp = dot(do, v, 1, 1)
        delta = jnp.sum(p * dp, axis=1, keepdims=True)
        ds = (p * (dp - delta) * scale).astype(jnp.bfloat16)
        gq = dot(ds, k, 1, 0).astype(jnp.bfloat16)
        grads_ref[i * steps : (i + 1) * steps, 0] = gq.reshape(steps, BLOCK, HEAD)
        gk = dot(q, ds, 0, 0)
        gv = dot(do, p.astype(jnp.bfloat16), 0, 0)
        if i:
            gk_ref[:, : width - ROWS] += gk[:, : width - ROWS]
            gv_ref[:, : width - ROWS] += gv[:, : width - ROWS]
            gk, gv = gk[:, width - ROWS :], gv[:, width - ROWS :]
        gk_ref[:, rows] = gk
        gv_ref[:, rows] = gv
    grads_ref[:, 1] = gk_ref[...].T.astype(jnp.bfloat16).reshape(n_tm, BLOCK, HEAD)
    grads_ref[:, 2] = gv_ref[...].T.astype(jnp.bfloat16).reshape(n_tm, BLOCK, HEAD)


VMEM = pl.BlockSpec(memory_space=pltpu.VMEM)
PARAMS = pltpu.CompilerParams(vmem_limit_bytes=48 * 1024 * 1024)


def cost(products, length, bytes_accessed):
    return pl.CostEstimate(
        flops=2 * products * length * length * HEAD,
        bytes_accessed=bytes_accessed,
        transcendentals=length * length,
    )


def forward(qkv):
    length = qkv.shape[0] * BLOCK
    return pl.pallas_call(
        forward_kernel,
        out_shape=(
            jax.ShapeDtypeStruct((length, HEAD), jnp.bfloat16),
            jax.ShapeDtypeStruct((length, 1), jnp.float32),
        ),
        in_specs=[VMEM],
        out_specs=(VMEM, VMEM),
        compiler_params=PARAMS,
        cost_estimate=cost(2, length, 2 << 20),
        name="forward",
    )(qkv)


def weight_term(att, places, pieces, norm_factor):
    length, width = att.shape[0], pieces[0].shape[1]
    half = jax.ShapeDtypeStruct((HEAD // 2, width), jnp.float32)
    return pl.pallas_call(
        functools.partial(weight_kernel, norm_factor, places),
        out_shape=(half, half),
        in_specs=[VMEM] * (1 + len(pieces)),
        out_specs=(VMEM, VMEM),
        scratch_shapes=[pltpu.VMEM((HEAD, width), jnp.float32)],
        compiler_params=PARAMS,
        cost_estimate=cost(1, length, 3 << 20),
        name="weight_term",
    )(att, *pieces)


def backward(qkv, lse, places, pieces, weight):
    length = lse.shape[0]
    return pl.pallas_call(
        functools.partial(backward_kernel, places),
        out_shape=jax.ShapeDtypeStruct(qkv.shape, jnp.bfloat16),
        in_specs=[VMEM] * (2 + len(pieces) + len(weight)),
        out_specs=VMEM,
        scratch_shapes=[
            pltpu.VMEM((pieces[0].shape[1], HEAD), jnp.bfloat16),
            pltpu.VMEM((length, HEAD), jnp.bfloat16),
            pltpu.VMEM((HEAD, length), jnp.float32),
            pltpu.VMEM((HEAD, length), jnp.float32),
        ],
        compiler_params=PARAMS,
        cost_estimate=cost(6, length, 4 << 20),
        name="backward",
    )(qkv, lse, *pieces, *weight)


def shuffle(inverse, flip):
    near = lax.broadcasted_iota(jnp.int32, (2 * BLOCK, 2 * BLOCK), 1 if inverse else 0)
    far = lax.broadcasted_iota(jnp.int32, (2 * BLOCK, 2 * BLOCK), 0 if inverse else 1)
    score = (near // BLOCK) ^ flip
    return jnp.where(far == 2 * (near % BLOCK) + score, 1.0, 0.0).astype(jnp.bfloat16)


def prepare_kernel(query_ref, key_ref, value_ref, grad_ref, out_ref, mine_ref, other_ref):
    parts = dot(shuffle(False, lax.axis_index("tm") % 2), grad_ref[...].reshape(2 * BLOCK, -1), 1, 0)
    mine_ref[...] = parts[:BLOCK].astype(jnp.bfloat16)
    other_ref[...] = parts[BLOCK:].astype(jnp.bfloat16)
    move = shuffle(False, 0)
    for a, ref in enumerate((query_ref, key_ref, value_ref)):
        rows = ref[...].reshape(2 * BLOCK, ref.shape[2])
        parts = dot(move, rows, 1, 0).astype(jnp.bfloat16)
        for score in range(2):
            for head in range(HEADS):
                out_ref[2 * head + score, a] = parts[
                    score * BLOCK : (score + 1) * BLOCK, head * HEAD : (head + 1) * HEAD
                ]


def unpack_kernel(in_ref, query_ref, key_ref, value_ref):
    move = shuffle(True, 0)
    for a, ref in enumerate((query_ref, key_ref, value_ref)):
        parts = jnp.concatenate(
            [
                jnp.concatenate([in_ref[2 * head + score, a] for head in range(HEADS)], axis=1)
                for score in range(2)
            ],
            axis=0,
        )
        rows = dot(move, parts, 1, 0).astype(jnp.bfloat16)
        ref[...] = rows.reshape(ref.shape)


def prepare(query, key, value, grad):
    half = jax.ShapeDtypeStruct((grad.shape[0], grad.shape[2]), grad.dtype)
    return pl.pallas_call(
        prepare_kernel,
        out_shape=(jax.ShapeDtypeStruct((2 * HEADS, 3, BLOCK, HEAD), query.dtype), half, half),
        in_specs=[VMEM] * 4,
        out_specs=(VMEM,) * 3,
        name="prepare",
    )(query, key, value, grad)


def unpack(items):
    rows = jax.ShapeDtypeStruct((BLOCK, 2, HEADS * HEAD), items.dtype)
    return pl.pallas_call(
        unpack_kernel, out_shape=(rows,) * 3, in_specs=[VMEM], out_specs=(VMEM,) * 3, name="unpack"
    )(items)


def swap(array, axis, mask):
    return lax.ppermute(array, axis, [(i, i ^ mask) for i in range(16)])


def shift(array, by):
    return lax.ppermute(array, "tm", [(i, (i + 4 * by) % 16) for i in range(16)])


def local(query_rows, key_rows, value_rows, grad_output, out_weight):
    step_rows, score_count, track_local, model_width = query_rows.shape
    n_tm = lax.axis_size("tm")
    total_tokens = step_rows * n_tm * score_count * track_local * lax.axis_size("track")
    norm_factor = 1.0 / math.sqrt(total_tokens)
    tm = lax.axis_index("tm")
    track = lax.axis_index("track")
    head = tm // 2

    flat = (step_rows, score_count, model_width)

    qkv, mine, other = prepare(*(a.reshape(flat) for a in (query_rows, key_rows, value_rows, grad_output)))
    chip_piece = jnp.concatenate([mine, swap(other, "tm", 1)], axis=0)
    far_piece = swap(chip_piece, "tm", 2)
    places, pieces = [], []
    for d in range(4):
        places.append((0, d))
        pieces.append(shift(chip_piece, d) if d else chip_piece)
    for d in range(4):
        places.append((1, d))
        pieces.append(shift(far_piece, d) if d else far_piece)

    held = lax.dynamic_slice_in_dim(out_weight.T, head * HEAD, HEAD, axis=1)
    held = jnp.concatenate([held] + [swap(held, "track", 4 * j) for j in (1, 2, 3)], axis=0)
    held_z = held
    held, _ = lax.optimization_barrier((held, far_piece))
    weight = [held] + [swap(held, "track", j) for j in (1, 2, 3)]

    qkv, _ = lax.optimization_barrier((qkv, (far_piece, held_z, pieces[1], pieces[2], pieces[3])))
    qkv = lax.all_to_all(qkv, "tm", split_axis=0, concat_axis=0, tiled=True)

    att, lse = forward(qkv)
    keep, send = weight_term(att, places, pieces, norm_factor)
    lse, _ = lax.optimization_barrier((lse, (keep, send)))

    total = keep + swap(send, "tm", 1)
    after_core = total
    total = total.reshape(4, 4, 4, model_width)
    for axis, step, place in ((1, 1, track % 4), (0, 4, track // 4)):
        parts = [lax.dynamic_index_in_dim(total, place ^ j, axis, keepdims=False) for j in range(4)]
        total = parts[0]
        for j in (1, 2, 3):
            total = total + swap(parts[j], "track", step * j)
        if step == 1:
            after_y = total
    grad_weight = total

    item_grads = backward(qkv, lse, places, pieces, weight)
    returned = lax.all_to_all(item_grads, "tm", split_axis=0, concat_axis=0, tiled=True)
    shape = query_rows.shape
    grad_query, grad_key, grad_value = (g.reshape(shape) for g in unpack(returned))
    return (grad_query, grad_key, grad_value, grad_weight)


def solution(mesh):
    return jax.shard_map(
        local,
        mesh=mesh,
        in_specs=(
            P("tm", None, "track", None),
            P("tm", None, "track", None),
            P("tm", None, "track", None),
            P("tm", None, "track", None),
            P(None, "track"),
        ),
        out_specs=(
            P("tm", None, "track", None),
            P("tm", None, "track", None),
            P("tm", None, "track", None),
            P(("tm", "track"), None),
        ),
        check_vma=False,
    )
```

```python
import functools
import math

import jax
import jax.numpy as jnp
from jax import lax
from jax.experimental import pallas as pl
from jax.experimental.pallas import tpu as pltpu
from jax.sharding import PartitionSpec as P

HEADS = 8
HEAD = 128
BLOCK = 64
ROWS = 256


def dot(a, b, ca, cb):
    return lax.dot_general(
        a, b, (((ca,), (cb,)), ((), ())), preferred_element_type=jnp.float32
    )


def logits_of(qkv_ref, i):
    steps = ROWS // BLOCK
    width = (i + 1) * ROWS
    q = qkv_ref[i * steps : (i + 1) * steps, 0].reshape(ROWS, HEAD)
    k = qkv_ref[: (i + 1) * steps, 1].reshape(width, HEAD)
    v = qkv_ref[: (i + 1) * steps, 2].reshape(width, HEAD)
    s = dot(q, k, 1, 1) * (HEAD ** (-0.5) * math.log2(math.e))
    row_at = lax.broadcasted_iota(jnp.int32, s.shape, 0) + i * ROWS
    col_at = lax.broadcasted_iota(jnp.int32, s.shape, 1)
    return jnp.where(col_at <= row_at, s, -1e30), q, k, v


def forward_kernel(qkv_ref, att_ref, lse_ref):
    for i in range(att_ref.shape[0] // ROWS):
        rows = slice(i * ROWS, (i + 1) * ROWS)
        s, _, _, v = logits_of(qkv_ref, i)
        peak = jnp.max(s, axis=1, keepdims=True)
        e = jnp.exp2(s - peak)
        total = jnp.sum(e, axis=1, keepdims=True)
        p_low = (e * (1.0 / total)).astype(jnp.bfloat16)
        att_ref[rows, :] = dot(p_low, v, 1, 0).astype(jnp.bfloat16)
        lse_ref[rows, :] = peak + jnp.log2(total)


def chunks(places, piece_refs):
    tm = lax.axis_index("tm")
    x, z, core = tm // 4, (tm // 2) % 2, tm % 2
    for (far, back), ref in zip(places, piece_refs):
        for at in range(ref.shape[0] // (2 * BLOCK)):
            chip_x = at if back is None else (x + 4 - back) % 4
            first = 4 * chip_x + 2 * (z ^ far)
            rows = [
                pl.ds(pl.multiple_of((first + (core ^ sub)) * BLOCK, BLOCK), BLOCK) for sub in range(2)
            ]
            yield ref[at * 2 * BLOCK : (at + 1) * 2 * BLOCK, :], rows


def weight_kernel(norm_factor, places, att_ref, *refs):
    keep_ref, send_ref, gw_ref = refs[len(places) :]
    core = lax.axis_index("tm") % 2
    for n, (chunk, rows) in enumerate(chunks(places, refs)):
        att = jnp.concatenate([att_ref[r, :] for r in rows], axis=0)
        term = dot(att, chunk, 0, 0)
        if n == 0:
            gw_ref[...] = term
        else:
            gw_ref[...] += term
    half = HEAD // 2
    keep_ref[...] = gw_ref[pl.ds(pl.multiple_of(core * half, half), half), :] * norm_factor
    send_ref[...] = gw_ref[pl.ds(pl.multiple_of((1 - core) * half, half), half), :] * norm_factor


def backward_kernel(places, qkv_ref, lse_ref, *refs):
    weight_refs = refs[len(places) : len(places) + 4]
    grads_ref, w_ref, do_ref, gk_ref, gv_ref = refs[len(places) + 4 :]
    n_tm = qkv_ref.shape[0]
    length = n_tm * BLOCK

    track = lax.axis_index("track")
    size = w_ref.shape[0] // 16
    for p in range(16):
        owner = track ^ ((p % 4) * 4 + p // 4)
        w_ref[pl.ds(pl.multiple_of(owner * size, size), size), :] = weight_refs[p // 4][
            (p % 4) * size : (p % 4 + 1) * size, :
        ]
    for chunk, rows in chunks(places, refs):
        part = dot(chunk, w_ref[...], 1, 0).astype(jnp.bfloat16)
        do_ref[rows[0], :] = part[:BLOCK]
        do_ref[rows[1], :] = part[BLOCK:]

    scale = HEAD ** (-0.5)
    steps = ROWS // BLOCK
    for i in range(length // ROWS):
        width = (i + 1) * ROWS
        rows = slice(i * ROWS, (i + 1) * ROWS)
        do = do_ref[rows, :]
        s, q, k, v = logits_of(qkv_ref, i)
        p = jnp.exp2(s - lse_ref[rows, :])
        dp = dot(do, v, 1, 1)
        delta = jnp.sum(p * dp, axis=1, keepdims=True)
        ds = (p * (dp - delta) * scale).astype(jnp.bfloat16)
        gq = dot(ds, k, 1, 0).astype(jnp.bfloat16)
        grads_ref[i * steps : (i + 1) * steps, 0] = gq.reshape(steps, BLOCK, HEAD)
        gk = dot(q, ds, 0, 0)
        gv = dot(do, p.astype(jnp.bfloat16), 0, 0)
        if i:
            gk_ref[:, : width - ROWS] += gk[:, : width - ROWS]
            gv_ref[:, : width - ROWS] += gv[:, : width - ROWS]
            gk, gv = gk[:, width - ROWS :], gv[:, width - ROWS :]
        gk_ref[:, rows] = gk
        gv_ref[:, rows] = gv
    grads_ref[:, 1] = gk_ref[...].T.astype(jnp.bfloat16).reshape(n_tm, BLOCK, HEAD)
    grads_ref[:, 2] = gv_ref[...].T.astype(jnp.bfloat16).reshape(n_tm, BLOCK, HEAD)


VMEM = pl.BlockSpec(memory_space=pltpu.VMEM)
PARAMS = pltpu.CompilerParams(vmem_limit_bytes=48 * 1024 * 1024)


def cost(products, length, bytes_accessed):
    return pl.CostEstimate(
        flops=2 * products * length * length * HEAD,
        bytes_accessed=bytes_accessed,
        transcendentals=length * length,
    )


def forward(qkv):
    length = qkv.shape[0] * BLOCK
    return pl.pallas_call(
        forward_kernel,
        out_shape=(
            jax.ShapeDtypeStruct((length, HEAD), jnp.bfloat16),
            jax.ShapeDtypeStruct((length, 1), jnp.float32),
        ),
        in_specs=[VMEM],
        out_specs=(VMEM, VMEM),
        compiler_params=PARAMS,
        cost_estimate=cost(2, length, 2 << 20),
        name="forward",
    )(qkv)


def weight_term(att, places, pieces, norm_factor):
    length, width = att.shape[0], pieces[0].shape[1]
    half = jax.ShapeDtypeStruct((HEAD // 2, width), jnp.float32)
    return pl.pallas_call(
        functools.partial(weight_kernel, norm_factor, places),
        out_shape=(half, half),
        in_specs=[VMEM] * (1 + len(pieces)),
        out_specs=(VMEM, VMEM),
        scratch_shapes=[pltpu.VMEM((HEAD, width), jnp.float32)],
        compiler_params=PARAMS,
        cost_estimate=cost(1, length, 3 << 20),
        name="weight_term",
    )(att, *pieces)


def backward(qkv, lse, places, pieces, weight):
    length = lse.shape[0]
    return pl.pallas_call(
        functools.partial(backward_kernel, places),
        out_shape=jax.ShapeDtypeStruct(qkv.shape, jnp.bfloat16),
        in_specs=[VMEM] * (2 + len(pieces) + len(weight)),
        out_specs=VMEM,
        scratch_shapes=[
            pltpu.VMEM((pieces[0].shape[1], HEAD), jnp.bfloat16),
            pltpu.VMEM((length, HEAD), jnp.bfloat16),
            pltpu.VMEM((HEAD, length), jnp.float32),
            pltpu.VMEM((HEAD, length), jnp.float32),
        ],
        compiler_params=PARAMS,
        cost_estimate=cost(6, length, 4 << 20),
        name="backward",
    )(qkv, lse, *pieces, *weight)


def shuffle(inverse, flip):
    near = lax.broadcasted_iota(jnp.int32, (2 * BLOCK, 2 * BLOCK), 1 if inverse else 0)
    far = lax.broadcasted_iota(jnp.int32, (2 * BLOCK, 2 * BLOCK), 0 if inverse else 1)
    score = (near // BLOCK) ^ flip
    return jnp.where(far == 2 * (near % BLOCK) + score, 1.0, 0.0).astype(jnp.bfloat16)


def prepare_kernel(query_ref, key_ref, value_ref, grad_ref, out_ref, mine_ref, other_ref):
    parts = dot(shuffle(False, lax.axis_index("tm") % 2), grad_ref[...].reshape(2 * BLOCK, -1), 1, 0)
    mine_ref[...] = parts[:BLOCK].astype(jnp.bfloat16)
    other_ref[...] = parts[BLOCK:].astype(jnp.bfloat16)
    move = shuffle(False, 0)
    for a, ref in enumerate((query_ref, key_ref, value_ref)):
        rows = ref[...].reshape(2 * BLOCK, ref.shape[2])
        parts = dot(move, rows, 1, 0).astype(jnp.bfloat16)
        for score in range(2):
            for head in range(HEADS):
                out_ref[2 * head + score, a] = parts[
                    score * BLOCK : (score + 1) * BLOCK, head * HEAD : (head + 1) * HEAD
                ]


def split_scores_kernel(rows_ref, mine_ref, other_ref):
    parts = dot(shuffle(False, lax.axis_index("tm") % 2), rows_ref[...].reshape(2 * BLOCK, -1), 1, 0)
    mine_ref[...] = parts[:BLOCK].astype(jnp.bfloat16)
    other_ref[...] = parts[BLOCK:].astype(jnp.bfloat16)


def unpack_kernel(in_ref, query_ref, key_ref, value_ref):
    move = shuffle(True, 0)
    for a, ref in enumerate((query_ref, key_ref, value_ref)):
        parts = jnp.concatenate(
            [
                jnp.concatenate([in_ref[2 * head + score, a] for head in range(HEADS)], axis=1)
                for score in range(2)
            ],
            axis=0,
        )
        rows = dot(move, parts, 1, 0).astype(jnp.bfloat16)
        ref[...] = rows.reshape(ref.shape)


def prepare(query, key, value, grad):
    half = jax.ShapeDtypeStruct((grad.shape[0], grad.shape[2]), grad.dtype)
    return pl.pallas_call(
        prepare_kernel,
        out_shape=(jax.ShapeDtypeStruct((2 * HEADS, 3, BLOCK, HEAD), query.dtype), half, half),
        in_specs=[VMEM] * 4,
        out_specs=(VMEM,) * 3,
        name="prepare",
    )(query, key, value, grad)


def split_scores(rows):
    half = jax.ShapeDtypeStruct((rows.shape[0], rows.shape[2]), rows.dtype)
    return pl.pallas_call(
        split_scores_kernel, out_shape=(half, half), in_specs=[VMEM], out_specs=(VMEM, VMEM), name="split_scores"
    )(rows)


def unpack(items):
    rows = jax.ShapeDtypeStruct((BLOCK, 2, HEADS * HEAD), items.dtype)
    return pl.pallas_call(
        unpack_kernel, out_shape=(rows,) * 3, in_specs=[VMEM], out_specs=(VMEM,) * 3, name="unpack"
    )(items)


def swap(array, axis, mask):
    return lax.ppermute(array, axis, [(i, i ^ mask) for i in range(16)])


def shift(array, by):
    return lax.ppermute(array, "tm", [(i, (i + 4 * by) % 16) for i in range(16)])


def local(query_rows, key_rows, value_rows, grad_output, out_weight):
    step_rows, score_count, track_local, model_width = query_rows.shape
    n_tm = lax.axis_size("tm")
    total_tokens = step_rows * n_tm * score_count * track_local * lax.axis_size("track")
    norm_factor = 1.0 / math.sqrt(total_tokens)
    tm = lax.axis_index("tm")
    track = lax.axis_index("track")
    head = tm // 2

    flat = (step_rows, score_count, model_width)

    qkv, mine, other = prepare(*(a.reshape(flat) for a in (query_rows, key_rows, value_rows, grad_output)))
    chip_piece = jnp.concatenate([mine, swap(other, "tm", 1)], axis=0)
    far_rows = swap(grad_output.reshape(flat), "tm", 2)
    places = [(far, back) for far in range(2) for back in range(4)]
    shifted = {2: shift(chip_piece, 2), 1: shift(chip_piece, 1), 3: shift(chip_piece, 3)}
    pieces = [chip_piece] + [shifted[d] for d in (1, 2, 3)]
    far_mine, far_other = split_scores(far_rows)
    far_piece = jnp.concatenate([far_mine, swap(far_other, "tm", 1)], axis=0)
    shifted = {2: shift(far_piece, 2), 1: shift(far_piece, 1), 3: shift(far_piece, 3)}
    pieces += [far_piece] + [shifted[d] for d in (1, 2, 3)]

    held = lax.dynamic_slice_in_dim(out_weight.T, head * HEAD, HEAD, axis=1)
    held, _ = lax.optimization_barrier((held, chip_piece))
    for mask in (4, 8):
        held = jnp.concatenate([held, swap(held, "track", mask)], axis=0)

    held_z = held
    held, _ = lax.optimization_barrier((held, far_rows))
    weight = [held] + [swap(held, "track", j) for j in (1, 2, 3)]

    qkv, _ = lax.optimization_barrier((qkv, (far_rows, held_z, pieces[1], pieces[2], pieces[3])))
    qkv = lax.all_to_all(qkv, "tm", split_axis=0, concat_axis=0, tiled=True)

    qkv, _ = lax.optimization_barrier((qkv, weight))
    att, lse = forward(qkv)
    keep, send = weight_term(att, places, pieces, norm_factor)
    lse, _ = lax.optimization_barrier((lse, (keep, send)))

    item_grads = backward(qkv, lse, places, pieces, weight)

    from_core = swap(send, "tm", 1)
    item_grads, from_core = lax.optimization_barrier((item_grads, from_core))
    total = keep + from_core
    total = total.reshape(4, 4, 4, model_width)
    for axis, step, place in ((1, 1, track % 4), (0, 4, track // 4)):
        parts = [lax.dynamic_index_in_dim(total, place ^ j, axis, keepdims=False) for j in range(4)]
        total = parts[0]
        for j in (1, 2, 3):
            total = total + swap(parts[j], "track", step * j)
        if step == 1:
            after_y = total
    grad_weight = total


    returned = lax.all_to_all(item_grads, "tm", split_axis=0, concat_axis=0, tiled=True)
    shape = query_rows.shape
    grad_query, grad_key, grad_value = (g.reshape(shape) for g in unpack(returned))
    return (grad_query, grad_key, grad_value, grad_weight)


def solution(mesh):
    return jax.shard_map(
        local,
        mesh=mesh,
        in_specs=(
            P("tm", None, "track", None),
            P("tm", None, "track", None),
            P("tm", None, "track", None),
            P("tm", None, "track", None),
            P(None, "track"),
        ),
        out_specs=(
            P("tm", None, "track", None),
            P("tm", None, "track", None),
            P("tm", None, "track", None),
            P(("tm", "track"), None),
        ),
        check_vma=False,
    )
```

```python
import functools
import math

import jax
import jax.numpy as jnp
from jax import lax
from jax.experimental import pallas as pl
from jax.experimental.pallas import tpu as pltpu
from jax.sharding import PartitionSpec as P

HEADS = 8
HEAD = 128
BLOCK = 64
ROWS = 256


def dot(a, b, ca, cb):
    return lax.dot_general(
        a, b, (((ca,), (cb,)), ((), ())), preferred_element_type=jnp.float32
    )


def logits_of(qkv_ref, i):
    steps = ROWS // BLOCK
    width = (i + 1) * ROWS
    q = qkv_ref[i * steps : (i + 1) * steps, 0].reshape(ROWS, HEAD)
    k = qkv_ref[: (i + 1) * steps, 1].reshape(width, HEAD)
    v = qkv_ref[: (i + 1) * steps, 2].reshape(width, HEAD)
    s = dot(q, k, 1, 1) * (HEAD ** (-0.5) * math.log2(math.e))
    row_at = lax.broadcasted_iota(jnp.int32, s.shape, 0) + i * ROWS
    col_at = lax.broadcasted_iota(jnp.int32, s.shape, 1)
    return jnp.where(col_at <= row_at, s, -1e30), q, k, v


def forward_kernel(qkv_ref, att_ref, lse_ref):
    for i in range(att_ref.shape[0] // ROWS):
        rows = slice(i * ROWS, (i + 1) * ROWS)
        s, _, _, v = logits_of(qkv_ref, i)
        peak = jnp.max(s, axis=1, keepdims=True)
        e = jnp.exp2(s - peak)
        total = jnp.sum(e, axis=1, keepdims=True)
        p_low = (e * (1.0 / total)).astype(jnp.bfloat16)
        att_ref[rows, :] = dot(p_low, v, 1, 0).astype(jnp.bfloat16)
        lse_ref[rows, :] = peak + jnp.log2(total)


def chunks(places, piece_refs):
    tm = lax.axis_index("tm")
    x, z, core = tm // 4, (tm // 2) % 2, tm % 2
    for (far, back), ref in zip(places, piece_refs):
        for at in range(ref.shape[0] // (2 * BLOCK)):
            chip_x = at if back is None else (x + 4 - back) % 4
            first = 4 * chip_x + 2 * (z ^ far)
            rows = [
                pl.ds(pl.multiple_of((first + (core ^ sub)) * BLOCK, BLOCK), BLOCK) for sub in range(2)
            ]
            yield ref[at * 2 * BLOCK : (at + 1) * 2 * BLOCK, :], rows


def weight_kernel(norm_factor, places, att_ref, *refs):
    keep_ref, send_ref, gw_ref = refs[len(places) :]
    core = lax.axis_index("tm") % 2
    for n, (chunk, rows) in enumerate(chunks(places, refs)):
        att = jnp.concatenate([att_ref[r, :] for r in rows], axis=0)
        term = dot(att, chunk, 0, 0)
        if n == 0:
            gw_ref[...] = term
        else:
            gw_ref[...] += term
    half = HEAD // 2
    keep_ref[...] = gw_ref[pl.ds(pl.multiple_of(core * half, half), half), :] * norm_factor
    send_ref[...] = gw_ref[pl.ds(pl.multiple_of((1 - core) * half, half), half), :] * norm_factor


def backward_kernel(places, qkv_ref, lse_ref, *refs):
    weight_refs = refs[len(places) : len(places) + 4]
    grads_ref, w_ref, do_ref, gk_ref, gv_ref = refs[len(places) + 4 :]
    n_tm = qkv_ref.shape[0]
    length = n_tm * BLOCK

    track = lax.axis_index("track")
    size = w_ref.shape[0] // 16
    for p in range(16):
        owner = track ^ ((p % 4) * 4 + p // 4)
        w_ref[pl.ds(pl.multiple_of(owner * size, size), size), :] = weight_refs[p // 4][
            (p % 4) * size : (p % 4 + 1) * size, :
        ]
    for chunk, rows in chunks(places, refs):
        part = dot(chunk, w_ref[...], 1, 0).astype(jnp.bfloat16)
        do_ref[rows[0], :] = part[:BLOCK]
        do_ref[rows[1], :] = part[BLOCK:]

    scale = HEAD ** (-0.5)
    steps = ROWS // BLOCK
    for i in range(length // ROWS):
        width = (i + 1) * ROWS
        rows = slice(i * ROWS, (i + 1) * ROWS)
        do = do_ref[rows, :]
        s, q, k, v = logits_of(qkv_ref, i)
        p = jnp.exp2(s - lse_ref[rows, :])
        dp = dot(do, v, 1, 1)
        delta = jnp.sum(p * dp, axis=1, keepdims=True)
        ds = (p * (dp - delta) * scale).astype(jnp.bfloat16)
        gq = dot(ds, k, 1, 0).astype(jnp.bfloat16)
        grads_ref[i * steps : (i + 1) * steps, 0] = gq.reshape(steps, BLOCK, HEAD)
        gk = dot(q, ds, 0, 0)
        gv = dot(do, p.astype(jnp.bfloat16), 0, 0)
        if i:
            gk_ref[:, : width - ROWS] += gk[:, : width - ROWS]
            gv_ref[:, : width - ROWS] += gv[:, : width - ROWS]
            gk, gv = gk[:, width - ROWS :], gv[:, width - ROWS :]
        gk_ref[:, rows] = gk
        gv_ref[:, rows] = gv
    grads_ref[:, 1] = gk_ref[...].T.astype(jnp.bfloat16).reshape(n_tm, BLOCK, HEAD)
    grads_ref[:, 2] = gv_ref[...].T.astype(jnp.bfloat16).reshape(n_tm, BLOCK, HEAD)


VMEM = pl.BlockSpec(memory_space=pltpu.VMEM)
PARAMS = pltpu.CompilerParams(vmem_limit_bytes=32 * 1024 * 1024)
SMALL = pltpu.CompilerParams(vmem_limit_bytes=16 * 1024 * 1024)


def cost(products, length, bytes_accessed):
    return pl.CostEstimate(
        flops=2 * products * length * length * HEAD,
        bytes_accessed=bytes_accessed,
        transcendentals=length * length,
    )


def forward(qkv):
    length = qkv.shape[0] * BLOCK
    return pl.pallas_call(
        forward_kernel,
        out_shape=(
            jax.ShapeDtypeStruct((length, HEAD), jnp.bfloat16),
            jax.ShapeDtypeStruct((length, 1), jnp.float32),
        ),
        in_specs=[VMEM],
        out_specs=(VMEM, VMEM),
        compiler_params=PARAMS,
        cost_estimate=cost(2, length, 2 << 20),
        name="forward",
    )(qkv)


def weight_term(att, places, pieces, norm_factor):
    length, width = att.shape[0], pieces[0].shape[1]
    half = jax.ShapeDtypeStruct((HEAD // 2, width), jnp.float32)
    return pl.pallas_call(
        functools.partial(weight_kernel, norm_factor, places),
        out_shape=(half, half),
        in_specs=[VMEM] * (1 + len(pieces)),
        out_specs=(VMEM, VMEM),
        scratch_shapes=[pltpu.VMEM((HEAD, width), jnp.float32)],
        compiler_params=PARAMS,
        cost_estimate=cost(1, length, 3 << 20),
        name="weight_term",
    )(att, *pieces)


def backward(qkv, lse, places, pieces, weight):
    length = lse.shape[0]
    return pl.pallas_call(
        functools.partial(backward_kernel, places),
        out_shape=jax.ShapeDtypeStruct(qkv.shape, jnp.bfloat16),
        in_specs=[VMEM] * (2 + len(pieces) + len(weight)),
        out_specs=VMEM,
        scratch_shapes=[
            pltpu.VMEM((pieces[0].shape[1], HEAD), jnp.bfloat16),
            pltpu.VMEM((length, HEAD), jnp.bfloat16),
            pltpu.VMEM((HEAD, length), jnp.float32),
            pltpu.VMEM((HEAD, length), jnp.float32),
        ],
        compiler_params=PARAMS,
        cost_estimate=cost(6, length, 4 << 20),
        name="backward",
    )(qkv, lse, *pieces, *weight)


def shuffle(inverse, flip):
    near = lax.broadcasted_iota(jnp.int32, (2 * BLOCK, 2 * BLOCK), 1 if inverse else 0)
    far = lax.broadcasted_iota(jnp.int32, (2 * BLOCK, 2 * BLOCK), 0 if inverse else 1)
    score = (near // BLOCK) ^ flip
    return jnp.where(far == 2 * (near % BLOCK) + score, 1.0, 0.0).astype(jnp.bfloat16)


def prepare_kernel(query_ref, key_ref, value_ref, grad_ref, out_ref, mine_ref, other_ref):
    parts = dot(shuffle(False, lax.axis_index("tm") % 2), grad_ref[...].reshape(2 * BLOCK, -1), 1, 0)
    mine_ref[...] = parts[:BLOCK].astype(jnp.bfloat16)
    other_ref[...] = parts[BLOCK:].astype(jnp.bfloat16)
    move = shuffle(False, 0)
    for a, ref in enumerate((query_ref, key_ref, value_ref)):
        rows = ref[...].reshape(2 * BLOCK, ref.shape[2])
        parts = dot(move, rows, 1, 0).astype(jnp.bfloat16)
        for score in range(2):
            for head in range(HEADS):
                out_ref[2 * head + score, a] = parts[
                    score * BLOCK : (score + 1) * BLOCK, head * HEAD : (head + 1) * HEAD
                ]


def split_scores_kernel(rows_ref, mine_ref, other_ref):
    parts = dot(shuffle(False, lax.axis_index("tm") % 2), rows_ref[...].reshape(2 * BLOCK, -1), 1, 0)
    mine_ref[...] = parts[:BLOCK].astype(jnp.bfloat16)
    other_ref[...] = parts[BLOCK:].astype(jnp.bfloat16)


def unpack_kernel(in_ref, query_ref, key_ref, value_ref):
    move = shuffle(True, 0)
    for a, ref in enumerate((query_ref, key_ref, value_ref)):
        parts = jnp.concatenate(
            [
                jnp.concatenate([in_ref[2 * head + score, a] for head in range(HEADS)], axis=1)
                for score in range(2)
            ],
            axis=0,
        )
        rows = dot(move, parts, 1, 0).astype(jnp.bfloat16)
        ref[...] = rows.reshape(ref.shape)


def prepare(query, key, value, grad):
    half = jax.ShapeDtypeStruct((grad.shape[0], grad.shape[2]), grad.dtype)
    return pl.pallas_call(
        prepare_kernel,
        out_shape=(jax.ShapeDtypeStruct((2 * HEADS, 3, BLOCK, HEAD), query.dtype), half, half),
        in_specs=[VMEM] * 4,
        out_specs=(VMEM,) * 3,
        name="prepare",
    )(query, key, value, grad)


def split_scores(rows):
    half = jax.ShapeDtypeStruct((rows.shape[0], rows.shape[2]), rows.dtype)
    return pl.pallas_call(
        split_scores_kernel, out_shape=(half, half), in_specs=[VMEM], out_specs=(VMEM, VMEM), compiler_params=SMALL, name="split_scores"
    )(rows)


def unpack(items):
    rows = jax.ShapeDtypeStruct((BLOCK, 2, HEADS * HEAD), items.dtype)
    return pl.pallas_call(
        unpack_kernel, out_shape=(rows,) * 3, in_specs=[VMEM], out_specs=(VMEM,) * 3, compiler_params=SMALL, name="unpack"
    )(items)


def swap(array, axis, mask):
    return lax.ppermute(array, axis, [(i, i ^ mask) for i in range(16)])


def shift(array, by):
    return lax.ppermute(array, "tm", [(i, (i + 4 * by) % 16) for i in range(16)])


def local(query_rows, key_rows, value_rows, grad_output, out_weight):
    step_rows, score_count, track_local, model_width = query_rows.shape
    n_tm = lax.axis_size("tm")
    total_tokens = step_rows * n_tm * score_count * track_local * lax.axis_size("track")
    norm_factor = 1.0 / math.sqrt(total_tokens)
    tm = lax.axis_index("tm")
    track = lax.axis_index("track")
    head = tm // 2

    flat = (step_rows, score_count, model_width)

    qkv, mine, other = prepare(*(a.reshape(flat) for a in (query_rows, key_rows, value_rows, grad_output)))
    chip_piece = jnp.concatenate([mine, swap(other, "tm", 1)], axis=0)
    far_rows = swap(grad_output.reshape(flat), "tm", 2)
    places = [(far, back) for far in range(2) for back in range(4)]
    shifted = {2: shift(chip_piece, 2), 1: shift(chip_piece, 1), 3: shift(chip_piece, 3)}
    pieces = [chip_piece] + [shifted[d] for d in (1, 2, 3)]
    far_mine, far_other = split_scores(far_rows)
    far_piece = jnp.concatenate([far_mine, swap(far_other, "tm", 1)], axis=0)
    shifted = {2: shift(far_piece, 2), 1: shift(far_piece, 1), 3: shift(far_piece, 3)}
    pieces += [far_piece] + [shifted[d] for d in (1, 2, 3)]

    held = lax.dynamic_slice_in_dim(out_weight.T, head * HEAD, HEAD, axis=1)
    held, _ = lax.optimization_barrier((held, chip_piece))
    for mask in (4, 8):
        held = jnp.concatenate([held, swap(held, "track", mask)], axis=0)

    held_z = held
    held, _ = lax.optimization_barrier((held, far_rows))
    weight = [held] + [swap(held, "track", j) for j in (1, 2, 3)]

    qkv, _ = lax.optimization_barrier((qkv, (far_mine, held_z, pieces[1], pieces[2], pieces[3])))
    qkv = lax.all_to_all(qkv, "tm", split_axis=0, concat_axis=0, tiled=True)

    qkv, _ = lax.optimization_barrier((qkv, weight))
    att, lse = forward(qkv)
    keep, send = weight_term(att, places, pieces, norm_factor)
    lse, _ = lax.optimization_barrier((lse, (keep, send)))

    item_grads = backward(qkv, lse, places, pieces, weight)

    from_core = swap(send, "tm", 1)
    item_grads, from_core = lax.optimization_barrier((item_grads, from_core))
    total = keep + from_core
    total = total.reshape(4, 4, 4, model_width)
    for axis, step, place in ((1, 1, track % 4), (0, 4, track // 4)):
        parts = [lax.dynamic_index_in_dim(total, place ^ j, axis, keepdims=False) for j in range(4)]
        total = parts[0]
        for j in (1, 2, 3):
            total = total + swap(parts[j], "track", step * j)
        if step == 1:
            after_y = total
    grad_weight = total


    returned = lax.all_to_all(item_grads, "tm", split_axis=0, concat_axis=0, tiled=True)
    shape = query_rows.shape
    grad_query, grad_key, grad_value = (g.reshape(shape) for g in unpack(returned))
    return (grad_query, grad_key, grad_value, grad_weight)


def solution(mesh):
    return jax.shard_map(
        local,
        mesh=mesh,
        in_specs=(
            P("tm", None, "track", None),
            P("tm", None, "track", None),
            P("tm", None, "track", None),
            P("tm", None, "track", None),
            P(None, "track"),
        ),
        out_specs=(
            P("tm", None, "track", None),
            P("tm", None, "track", None),
            P("tm", None, "track", None),
            P(("tm", "track"), None),
        ),
        check_vma=False,
    )
```

```python
import functools
import math

import jax
import jax.numpy as jnp
from jax import lax
from jax.experimental import pallas as pl
from jax.experimental.pallas import tpu as pltpu
from jax.sharding import PartitionSpec as P

HEADS = 8
HEAD = 128
BLOCK = 64
ROWS = 256


def dot(a, b, ca, cb):
    return lax.dot_general(
        a, b, (((ca,), (cb,)), ((), ())), preferred_element_type=jnp.float32
    )


def logits_of(qkv_ref, i):
    steps = ROWS // BLOCK
    width = (i + 1) * ROWS
    q = qkv_ref[i * steps : (i + 1) * steps, 0].reshape(ROWS, HEAD)
    k = qkv_ref[: (i + 1) * steps, 1].reshape(width, HEAD)
    v = qkv_ref[: (i + 1) * steps, 2].reshape(width, HEAD)
    s = dot(q, k, 1, 1) * (HEAD ** (-0.5) * math.log2(math.e))
    row_at = lax.broadcasted_iota(jnp.int32, s.shape, 0) + i * ROWS
    col_at = lax.broadcasted_iota(jnp.int32, s.shape, 1)
    return jnp.where(col_at <= row_at, s, -1e30), q, k, v


def forward_kernel(qkv_ref, att_ref, lse_ref):
    for i in range(att_ref.shape[0] // ROWS):
        rows = slice(i * ROWS, (i + 1) * ROWS)
        s, _, _, v = logits_of(qkv_ref, i)
        peak = jnp.max(s, axis=1, keepdims=True)
        e = jnp.exp2(s - peak)
        total = jnp.sum(e, axis=1, keepdims=True)
        p_low = (e * (1.0 / total)).astype(jnp.bfloat16)
        att_ref[rows, :] = dot(p_low, v, 1, 0).astype(jnp.bfloat16)
        lse_ref[rows, :] = peak + jnp.log2(total)


def chunks(places, piece_refs):
    tm = lax.axis_index("tm")
    x, z, core = tm // 4, (tm // 2) % 2, tm % 2
    for (far, back), ref in zip(places, piece_refs):
        for at in range(ref.shape[0] // (2 * BLOCK)):
            chip_x = at if back is None else (x + 4 - back) % 4
            first = 4 * chip_x + 2 * (z ^ far)
            rows = [
                pl.ds(pl.multiple_of((first + (core ^ sub)) * BLOCK, BLOCK), BLOCK) for sub in range(2)
            ]
            yield ref[at * 2 * BLOCK : (at + 1) * 2 * BLOCK, :], rows


def weight_kernel(norm_factor, places, att_ref, *refs):
    keep_ref, send_ref, gw_ref = refs[len(places) :]
    core = lax.axis_index("tm") % 2
    for n, (chunk, rows) in enumerate(chunks(places, refs)):
        att = jnp.concatenate([att_ref[r, :] for r in rows], axis=0)
        term = dot(att, chunk, 0, 0)
        if n == 0:
            gw_ref[...] = term
        else:
            gw_ref[...] += term
    half = HEAD // 2
    keep_ref[...] = gw_ref[pl.ds(pl.multiple_of(core * half, half), half), :] * norm_factor
    send_ref[...] = gw_ref[pl.ds(pl.multiple_of((1 - core) * half, half), half), :] * norm_factor


def backward_kernel(places, qkv_ref, lse_ref, *refs):
    weight_refs = refs[len(places) : len(places) + 4]
    grads_ref, w_ref, do_ref, gk_ref, gv_ref = refs[len(places) + 4 :]
    n_tm = qkv_ref.shape[0]
    length = n_tm * BLOCK

    track = lax.axis_index("track")
    size = w_ref.shape[0] // 16
    for p in range(16):
        owner = track ^ ((p % 4) * 4 + p // 4)
        w_ref[pl.ds(pl.multiple_of(owner * size, size), size), :] = weight_refs[p // 4][
            (p % 4) * size : (p % 4 + 1) * size, :
        ]
    for chunk, rows in chunks(places, refs):
        part = dot(chunk, w_ref[...], 1, 0).astype(jnp.bfloat16)
        do_ref[rows[0], :] = part[:BLOCK]
        do_ref[rows[1], :] = part[BLOCK:]

    scale = HEAD ** (-0.5)
    steps = ROWS // BLOCK
    for i in range(length // ROWS):
        width = (i + 1) * ROWS
        rows = slice(i * ROWS, (i + 1) * ROWS)
        do = do_ref[rows, :]
        s, q, k, v = logits_of(qkv_ref, i)
        p = jnp.exp2(s - lse_ref[rows, :])
        dp = dot(do, v, 1, 1)
        delta = jnp.sum(p * dp, axis=1, keepdims=True)
        ds = (p * (dp - delta) * scale).astype(jnp.bfloat16)
        gq = dot(ds, k, 1, 0).astype(jnp.bfloat16)
        grads_ref[i * steps : (i + 1) * steps, 0] = gq.reshape(steps, BLOCK, HEAD)
        gk = dot(q, ds, 0, 0)
        gv = dot(do, p.astype(jnp.bfloat16), 0, 0)
        if i:
            gk_ref[:, : width - ROWS] += gk[:, : width - ROWS]
            gv_ref[:, : width - ROWS] += gv[:, : width - ROWS]
            gk, gv = gk[:, width - ROWS :], gv[:, width - ROWS :]
        gk_ref[:, rows] = gk
        gv_ref[:, rows] = gv
    grads_ref[:, 1] = gk_ref[...].T.astype(jnp.bfloat16).reshape(n_tm, BLOCK, HEAD)
    grads_ref[:, 2] = gv_ref[...].T.astype(jnp.bfloat16).reshape(n_tm, BLOCK, HEAD)


VMEM = pl.BlockSpec(memory_space=pltpu.VMEM)
PARAMS = pltpu.CompilerParams(vmem_limit_bytes=32 * 1024 * 1024)
SMALL = pltpu.CompilerParams(vmem_limit_bytes=16 * 1024 * 1024)


def cost(products, length, bytes_accessed):
    return pl.CostEstimate(
        flops=2 * products * length * length * HEAD,
        bytes_accessed=bytes_accessed,
        transcendentals=length * length,
    )


def forward(qkv):
    length = qkv.shape[0] * BLOCK
    return pl.pallas_call(
        forward_kernel,
        out_shape=(
            jax.ShapeDtypeStruct((length, HEAD), jnp.bfloat16),
            jax.ShapeDtypeStruct((length, 1), jnp.float32),
        ),
        in_specs=[VMEM],
        out_specs=(VMEM, VMEM),
        compiler_params=PARAMS,
        cost_estimate=cost(2, length, 2 << 20),
        name="forward",
    )(qkv)


def weight_term(att, places, pieces, norm_factor):
    length, width = att.shape[0], pieces[0].shape[1]
    half = jax.ShapeDtypeStruct((HEAD // 2, width), jnp.float32)
    return pl.pallas_call(
        functools.partial(weight_kernel, norm_factor, places),
        out_shape=(half, half),
        in_specs=[VMEM] * (1 + len(pieces)),
        out_specs=(VMEM, VMEM),
        scratch_shapes=[pltpu.VMEM((HEAD, width), jnp.float32)],
        compiler_params=PARAMS,
        cost_estimate=cost(1, length, 3 << 20),
        name="weight_term",
    )(att, *pieces)


def backward(qkv, lse, places, pieces, weight):
    length = lse.shape[0]
    return pl.pallas_call(
        functools.partial(backward_kernel, places),
        out_shape=jax.ShapeDtypeStruct(qkv.shape, jnp.bfloat16),
        in_specs=[VMEM] * (2 + len(pieces) + len(weight)),
        out_specs=VMEM,
        scratch_shapes=[
            pltpu.VMEM((pieces[0].shape[1], HEAD), jnp.bfloat16),
            pltpu.VMEM((length, HEAD), jnp.bfloat16),
            pltpu.VMEM((HEAD, length), jnp.float32),
            pltpu.VMEM((HEAD, length), jnp.float32),
        ],
        compiler_params=PARAMS,
        cost_estimate=cost(6, length, 4 << 20),
        name="backward",
    )(qkv, lse, *pieces, *weight)


def shuffle(inverse, flip):
    near = lax.broadcasted_iota(jnp.int32, (2 * BLOCK, 2 * BLOCK), 1 if inverse else 0)
    far = lax.broadcasted_iota(jnp.int32, (2 * BLOCK, 2 * BLOCK), 0 if inverse else 1)
    score = (near // BLOCK) ^ flip
    return jnp.where(far == 2 * (near % BLOCK) + score, 1.0, 0.0).astype(jnp.bfloat16)


def prepare_kernel(query_ref, key_ref, value_ref, grad_ref, out_ref, mine_ref, other_ref):
    parts = dot(shuffle(False, lax.axis_index("tm") % 2), grad_ref[...].reshape(2 * BLOCK, -1), 1, 0)
    mine_ref[...] = parts[:BLOCK].astype(jnp.bfloat16)
    other_ref[...] = parts[BLOCK:].astype(jnp.bfloat16)
    move = shuffle(False, 0)
    for a, ref in enumerate((query_ref, key_ref, value_ref)):
        rows = ref[...].reshape(2 * BLOCK, ref.shape[2])
        parts = dot(move, rows, 1, 0).astype(jnp.bfloat16)
        for score in range(2):
            for head in range(HEADS):
                out_ref[2 * head + score, a] = parts[
                    score * BLOCK : (score + 1) * BLOCK, head * HEAD : (head + 1) * HEAD
                ]


def split_scores_kernel(rows_ref, mine_ref, other_ref):
    parts = dot(shuffle(False, lax.axis_index("tm") % 2), rows_ref[...].reshape(2 * BLOCK, -1), 1, 0)
    mine_ref[...] = parts[:BLOCK].astype(jnp.bfloat16)
    other_ref[...] = parts[BLOCK:].astype(jnp.bfloat16)


def unpack_kernel(in_ref, query_ref, key_ref, value_ref):
    move = shuffle(True, 0)
    for a, ref in enumerate((query_ref, key_ref, value_ref)):
        parts = jnp.concatenate(
            [
                jnp.concatenate([in_ref[2 * head + score, a] for head in range(HEADS)], axis=1)
                for score in range(2)
            ],
            axis=0,
        )
        rows = dot(move, parts, 1, 0).astype(jnp.bfloat16)
        ref[...] = rows.reshape(ref.shape)


def prepare(query, key, value, grad):
    half = jax.ShapeDtypeStruct((grad.shape[0], grad.shape[2]), grad.dtype)
    return pl.pallas_call(
        prepare_kernel,
        out_shape=(jax.ShapeDtypeStruct((2 * HEADS, 3, BLOCK, HEAD), query.dtype), half, half),
        in_specs=[VMEM] * 4,
        out_specs=(VMEM,) * 3,
        name="prepare",
    )(query, key, value, grad)


def split_scores(rows):
    half = jax.ShapeDtypeStruct((rows.shape[0], rows.shape[2]), rows.dtype)
    return pl.pallas_call(
        split_scores_kernel, out_shape=(half, half), in_specs=[VMEM], out_specs=(VMEM, VMEM), compiler_params=SMALL, name="split_scores"
    )(rows)


def unpack(items):
    rows = jax.ShapeDtypeStruct((BLOCK, 2, HEADS * HEAD), items.dtype)
    return pl.pallas_call(
        unpack_kernel, out_shape=(rows,) * 3, in_specs=[VMEM], out_specs=(VMEM,) * 3, compiler_params=SMALL, name="unpack"
    )(items)


def swap(array, axis, mask):
    return lax.ppermute(array, axis, [(i, i ^ mask) for i in range(16)])


def shift(array, by):
    return lax.ppermute(array, "tm", [(i, (i + 4 * by) % 16) for i in range(16)])


def local(query_rows, key_rows, value_rows, grad_output, out_weight):
    step_rows, score_count, track_local, model_width = query_rows.shape
    n_tm = lax.axis_size("tm")
    total_tokens = step_rows * n_tm * score_count * track_local * lax.axis_size("track")
    norm_factor = 1.0 / math.sqrt(total_tokens)
    tm = lax.axis_index("tm")
    track = lax.axis_index("track")
    head = tm // 2

    flat = (step_rows, score_count, model_width)

    qkv, mine, other = prepare(*(a.reshape(flat) for a in (query_rows, key_rows, value_rows, grad_output)))
    chip_piece = jnp.concatenate([mine, swap(other, "tm", 1)], axis=0)
    far_rows = swap(grad_output.reshape(flat), "tm", 2)
    places = [(far, back) for far in range(2) for back in range(4)]
    shifted = {2: shift(chip_piece, 2), 1: shift(chip_piece, 1), 3: shift(chip_piece, 3)}
    pieces = [chip_piece] + [shifted[d] for d in (1, 2, 3)]
    far_mine, far_other = split_scores(far_rows)
    far_piece = jnp.concatenate([far_mine, swap(far_other, "tm", 1)], axis=0)
    shifted = {2: shift(far_piece, 2), 1: shift(far_piece, 1), 3: shift(far_piece, 3)}
    pieces += [far_piece] + [shifted[d] for d in (1, 2, 3)]

    held = lax.dynamic_slice_in_dim(out_weight.T, head * HEAD, HEAD, axis=1)
    held, _ = lax.optimization_barrier((held, chip_piece))
    for mask in (4, 8):
        held = jnp.concatenate([held, swap(held, "track", mask)], axis=0)

    held_z = held
    held, _ = lax.optimization_barrier((held, far_rows))
    weight = [held] + [swap(held, "track", j) for j in (1, 2, 3)]

    qkv, _ = lax.optimization_barrier((qkv, (far_mine, held_z, pieces[1], pieces[2], pieces[3])))
    qkv = lax.all_to_all(qkv, "tm", split_axis=0, concat_axis=0, tiled=True)

    qkv, _ = lax.optimization_barrier((qkv, weight))
    att, lse = forward(qkv)
    keep, send = weight_term(att, places, pieces, norm_factor)

    item_grads = backward(qkv, lse, places, pieces, weight)

    from_core = swap(send, "tm", 1)
    terms = (keep, from_core)
    for rest, axis, step, place in (((4, 4, 4), 1, 1, track % 4), ((4, 4), 0, 4, track // 4)):
        terms = [term.reshape(rest + (model_width,)) for term in terms]
        parts = [
            sum(lax.dynamic_index_in_dim(term, place ^ j, axis, keepdims=False) for term in terms) for j in range(4)
        ]
        total = parts[0]
        for j in (1, 2, 3):
            total = total + swap(parts[j], "track", step * j)
        terms = (total,)
    grad_weight = total


    returned = lax.all_to_all(item_grads, "tm", split_axis=0, concat_axis=0, tiled=True)
    shape = query_rows.shape
    grad_query, grad_key, grad_value = (g.reshape(shape) for g in unpack(returned))
    return (grad_query, grad_key, grad_value, grad_weight)


def solution(mesh):
    return jax.shard_map(
        local,
        mesh=mesh,
        in_specs=(
            P("tm", None, "track", None),
            P("tm", None, "track", None),
            P("tm", None, "track", None),
            P("tm", None, "track", None),
            P(None, "track"),
        ),
        out_specs=(
            P("tm", None, "track", None),
            P("tm", None, "track", None),
            P("tm", None, "track", None),
            P(("tm", "track"), None),
        ),
        check_vma=False,
    )
```

```python
import functools
import math

import jax
import jax.numpy as jnp
from jax import lax
from jax.experimental import pallas as pl
from jax.experimental.pallas import tpu as pltpu
from jax.sharding import PartitionSpec as P

HEADS = 8
HEAD = 128
BLOCK = 64
ROWS = 512


def dot(a, b, ca, cb):
    return lax.dot_general(
        a, b, (((ca,), (cb,)), ((), ())), preferred_element_type=jnp.float32
    )


def logits_of(qkv_ref, i):
    steps = ROWS // BLOCK
    width = (i + 1) * ROWS
    q = qkv_ref[i * steps : (i + 1) * steps, 0].reshape(ROWS, HEAD)
    k = qkv_ref[: (i + 1) * steps, 1].reshape(width, HEAD)
    v = qkv_ref[: (i + 1) * steps, 2].reshape(width, HEAD)
    s = dot(q, k, 1, 1) * (HEAD ** (-0.5) * math.log2(math.e))
    row_at = lax.broadcasted_iota(jnp.int32, s.shape, 0) + i * ROWS
    col_at = lax.broadcasted_iota(jnp.int32, s.shape, 1)
    return jnp.where(col_at <= row_at, s, -1e30), q, k, v


def forward_kernel(qkv_ref, att_ref, lse_ref):
    for i in range(att_ref.shape[0] // ROWS):
        rows = slice(i * ROWS, (i + 1) * ROWS)
        s, _, _, v = logits_of(qkv_ref, i)
        peak = jnp.max(s, axis=1, keepdims=True)
        e = jnp.exp2(s - peak)
        total = jnp.sum(e, axis=1, keepdims=True)
        p_low = (e * (1.0 / total)).astype(jnp.bfloat16)
        att_ref[rows, :] = dot(p_low, v, 1, 0).astype(jnp.bfloat16)
        lse_ref[rows, :] = peak + jnp.log2(total)


def chunks(places, piece_refs):
    tm = lax.axis_index("tm")
    x, z, core = tm // 4, (tm // 2) % 2, tm % 2
    for (far, back), ref in zip(places, piece_refs):
        for at in range(ref.shape[0] // (2 * BLOCK)):
            chip_x = at if back is None else (x + 4 - back) % 4
            first = 4 * chip_x + 2 * (z ^ far)
            rows = [
                pl.ds(pl.multiple_of((first + (core ^ sub)) * BLOCK, BLOCK), BLOCK) for sub in range(2)
            ]
            yield ref[at * 2 * BLOCK : (at + 1) * 2 * BLOCK, :], rows


def weight_kernel(norm_factor, places, att_ref, *refs):
    keep_ref, send_ref, gw_ref = refs[len(places) :]
    core = lax.axis_index("tm") % 2
    for n, (chunk, rows) in enumerate(chunks(places, refs)):
        att = jnp.concatenate([att_ref[r, :] for r in rows], axis=0)
        term = dot(att, chunk, 0, 0)
        if n == 0:
            gw_ref[...] = term
        else:
            gw_ref[...] += term
    half = HEAD // 2
    keep_ref[...] = gw_ref[pl.ds(pl.multiple_of(core * half, half), half), :] * norm_factor
    send_ref[...] = gw_ref[pl.ds(pl.multiple_of((1 - core) * half, half), half), :] * norm_factor


def backward_kernel(places, qkv_ref, lse_ref, *refs):
    weight_refs = refs[len(places) : len(places) + 4]
    grads_ref, w_ref, do_ref, gk_ref, gv_ref = refs[len(places) + 4 :]
    n_tm = qkv_ref.shape[0]
    length = n_tm * BLOCK

    track = lax.axis_index("track")
    size = w_ref.shape[0] // 16
    for p in range(16):
        owner = track ^ ((p % 4) * 4 + p // 4)
        w_ref[pl.ds(pl.multiple_of(owner * size, size), size), :] = weight_refs[p // 4][
            (p % 4) * size : (p % 4 + 1) * size, :
        ]
    for chunk, rows in chunks(places, refs):
        part = dot(chunk, w_ref[...], 1, 0).astype(jnp.bfloat16)
        do_ref[rows[0], :] = part[:BLOCK]
        do_ref[rows[1], :] = part[BLOCK:]

    scale = HEAD ** (-0.5)
    steps = ROWS // BLOCK
    for i in range(length // ROWS):
        width = (i + 1) * ROWS
        rows = slice(i * ROWS, (i + 1) * ROWS)
        do = do_ref[rows, :]
        s, q, k, v = logits_of(qkv_ref, i)
        p = jnp.exp2(s - lse_ref[rows, :])
        dp = dot(do, v, 1, 1)
        delta = jnp.sum(p * dp, axis=1, keepdims=True)
        ds = (p * (dp - delta) * scale).astype(jnp.bfloat16)
        gq = dot(ds, k, 1, 0).astype(jnp.bfloat16)
        grads_ref[i * steps : (i + 1) * steps, 0] = gq.reshape(steps, BLOCK, HEAD)
        gk = dot(q, ds, 0, 0)
        gv = dot(do, p.astype(jnp.bfloat16), 0, 0)
        if i:
            gk_ref[:, : width - ROWS] += gk[:, : width - ROWS]
            gv_ref[:, : width - ROWS] += gv[:, : width - ROWS]
            gk, gv = gk[:, width - ROWS :], gv[:, width - ROWS :]
        gk_ref[:, rows] = gk
        gv_ref[:, rows] = gv
    grads_ref[:, 1] = gk_ref[...].T.astype(jnp.bfloat16).reshape(n_tm, BLOCK, HEAD)
    grads_ref[:, 2] = gv_ref[...].T.astype(jnp.bfloat16).reshape(n_tm, BLOCK, HEAD)


VMEM = pl.BlockSpec(memory_space=pltpu.VMEM)
PARAMS = pltpu.CompilerParams(vmem_limit_bytes=32 * 1024 * 1024)
SMALL = pltpu.CompilerParams(vmem_limit_bytes=16 * 1024 * 1024)


def cost(products, length, bytes_accessed):
    return pl.CostEstimate(
        flops=2 * products * length * length * HEAD,
        bytes_accessed=bytes_accessed,
        transcendentals=length * length,
    )


def forward(qkv):
    length = qkv.shape[0] * BLOCK
    return pl.pallas_call(
        forward_kernel,
        out_shape=(
            jax.ShapeDtypeStruct((length, HEAD), jnp.bfloat16),
            jax.ShapeDtypeStruct((length, 1), jnp.float32),
        ),
        in_specs=[VMEM],
        out_specs=(VMEM, VMEM),
        compiler_params=PARAMS,
        cost_estimate=cost(2, length, 2 << 20),
        name="forward",
    )(qkv)


def weight_term(att, places, pieces, norm_factor):
    length, width = att.shape[0], pieces[0].shape[1]
    half = jax.ShapeDtypeStruct((HEAD // 2, width), jnp.float32)
    return pl.pallas_call(
        functools.partial(weight_kernel, norm_factor, places),
        out_shape=(half, half),
        in_specs=[VMEM] * (1 + len(pieces)),
        out_specs=(VMEM, VMEM),
        scratch_shapes=[pltpu.VMEM((HEAD, width), jnp.float32)],
        compiler_params=PARAMS,
        cost_estimate=cost(1, length, 3 << 20),
        name="weight_term",
    )(att, *pieces)


def backward(qkv, lse, places, pieces, weight):
    length = lse.shape[0]
    return pl.pallas_call(
        functools.partial(backward_kernel, places),
        out_shape=jax.ShapeDtypeStruct(qkv.shape, jnp.bfloat16),
        in_specs=[VMEM] * (2 + len(pieces) + len(weight)),
        out_specs=VMEM,
        scratch_shapes=[
            pltpu.VMEM((pieces[0].shape[1], HEAD), jnp.bfloat16),
            pltpu.VMEM((length, HEAD), jnp.bfloat16),
            pltpu.VMEM((HEAD, length), jnp.float32),
            pltpu.VMEM((HEAD, length), jnp.float32),
        ],
        compiler_params=PARAMS,
        cost_estimate=cost(6, length, 4 << 20),
        name="backward",
    )(qkv, lse, *pieces, *weight)


def shuffle(inverse, flip):
    near = lax.broadcasted_iota(jnp.int32, (2 * BLOCK, 2 * BLOCK), 1 if inverse else 0)
    far = lax.broadcasted_iota(jnp.int32, (2 * BLOCK, 2 * BLOCK), 0 if inverse else 1)
    score = (near // BLOCK) ^ flip
    return jnp.where(far == 2 * (near % BLOCK) + score, 1.0, 0.0).astype(jnp.bfloat16)


def prepare_kernel(query_ref, key_ref, value_ref, grad_ref, out_ref, mine_ref, other_ref):
    parts = dot(shuffle(False, lax.axis_index("tm") % 2), grad_ref[...].reshape(2 * BLOCK, -1), 1, 0)
    mine_ref[...] = parts[:BLOCK].astype(jnp.bfloat16)
    other_ref[...] = parts[BLOCK:].astype(jnp.bfloat16)
    move = shuffle(False, 0)
    for a, ref in enumerate((query_ref, key_ref, value_ref)):
        rows = ref[...].reshape(2 * BLOCK, ref.shape[2])
        parts = dot(move, rows, 1, 0).astype(jnp.bfloat16)
        for score in range(2):
            for head in range(HEADS):
                out_ref[2 * head + score, a] = parts[
                    score * BLOCK : (score + 1) * BLOCK, head * HEAD : (head + 1) * HEAD
                ]


def split_scores_kernel(rows_ref, mine_ref, other_ref):
    parts = dot(shuffle(False, lax.axis_index("tm") % 2), rows_ref[...].reshape(2 * BLOCK, -1), 1, 0)
    mine_ref[...] = parts[:BLOCK].astype(jnp.bfloat16)
    other_ref[...] = parts[BLOCK:].astype(jnp.bfloat16)


def unpack_kernel(in_ref, query_ref, key_ref, value_ref):
    move = shuffle(True, 0)
    for a, ref in enumerate((query_ref, key_ref, value_ref)):
        parts = jnp.concatenate(
            [
                jnp.concatenate([in_ref[2 * head + score, a] for head in range(HEADS)], axis=1)
                for score in range(2)
            ],
            axis=0,
        )
        rows = dot(move, parts, 1, 0).astype(jnp.bfloat16)
        ref[...] = rows.reshape(ref.shape)


def prepare(query, key, value, grad):
    half = jax.ShapeDtypeStruct((grad.shape[0], grad.shape[2]), grad.dtype)
    return pl.pallas_call(
        prepare_kernel,
        out_shape=(jax.ShapeDtypeStruct((2 * HEADS, 3, BLOCK, HEAD), query.dtype), half, half),
        in_specs=[VMEM] * 4,
        out_specs=(VMEM,) * 3,
        name="prepare",
    )(query, key, value, grad)


def split_scores(rows):
    half = jax.ShapeDtypeStruct((rows.shape[0], rows.shape[2]), rows.dtype)
    return pl.pallas_call(
        split_scores_kernel, out_shape=(half, half), in_specs=[VMEM], out_specs=(VMEM, VMEM), compiler_params=SMALL, name="split_scores"
    )(rows)


def unpack(items):
    rows = jax.ShapeDtypeStruct((BLOCK, 2, HEADS * HEAD), items.dtype)
    return pl.pallas_call(
        unpack_kernel, out_shape=(rows,) * 3, in_specs=[VMEM], out_specs=(VMEM,) * 3, compiler_params=SMALL, name="unpack"
    )(items)


def swap(array, axis, mask):
    return lax.ppermute(array, axis, [(i, i ^ mask) for i in range(16)])


def shift(array, by):
    return lax.ppermute(array, "tm", [(i, (i + 4 * by) % 16) for i in range(16)])


def local(query_rows, key_rows, value_rows, grad_output, out_weight):
    step_rows, score_count, track_local, model_width = query_rows.shape
    n_tm = lax.axis_size("tm")
    total_tokens = step_rows * n_tm * score_count * track_local * lax.axis_size("track")
    norm_factor = 1.0 / math.sqrt(total_tokens)
    tm = lax.axis_index("tm")
    track = lax.axis_index("track")
    head = tm // 2

    flat = (step_rows, score_count, model_width)

    qkv, mine, other = prepare(*(a.reshape(flat) for a in (query_rows, key_rows, value_rows, grad_output)))
    chip_piece = jnp.concatenate([mine, swap(other, "tm", 1)], axis=0)
    far_rows = swap(grad_output.reshape(flat), "tm", 2)
    places = [(far, back) for far in range(2) for back in range(4)]
    shifted = {2: shift(chip_piece, 2), 1: shift(chip_piece, 1), 3: shift(chip_piece, 3)}
    pieces = [chip_piece] + [shifted[d] for d in (1, 2, 3)]
    far_mine, far_other = split_scores(far_rows)
    far_piece = jnp.concatenate([far_mine, swap(far_other, "tm", 1)], axis=0)
    shifted = {2: shift(far_piece, 2), 1: shift(far_piece, 1), 3: shift(far_piece, 3)}
    pieces += [far_piece] + [shifted[d] for d in (1, 2, 3)]

    held = lax.dynamic_slice_in_dim(out_weight.T, head * HEAD, HEAD, axis=1)
    held, _ = lax.optimization_barrier((held, chip_piece))
    for mask in (4, 8):
        held = jnp.concatenate([held, swap(held, "track", mask)], axis=0)

    held_z = held
    held, _ = lax.optimization_barrier((held, far_rows))
    weight = [held] + [swap(held, "track", j) for j in (1, 2, 3)]

    qkv, _ = lax.optimization_barrier((qkv, (far_mine, held_z, pieces[1], pieces[2], pieces[3])))
    qkv = lax.all_to_all(qkv, "tm", split_axis=0, concat_axis=0, tiled=True)

    qkv, _ = lax.optimization_barrier((qkv, weight))
    att, lse = forward(qkv)
    keep, send = weight_term(att, places, pieces, norm_factor)

    item_grads = backward(qkv, lse, places, pieces, weight)

    from_core = swap(send, "tm", 1)
    terms = (keep, from_core)
    for rest, axis, step, place in (((4, 4, 4), 1, 1, track % 4), ((4, 4), 0, 4, track // 4)):
        terms = [term.reshape(rest + (model_width,)) for term in terms]
        parts = [
            sum(lax.dynamic_index_in_dim(term, place ^ j, axis, keepdims=False) for term in terms) for j in range(4)
        ]
        total = parts[0]
        for j in (1, 2, 3):
            total = total + swap(parts[j], "track", step * j)
        terms = (total,)
    grad_weight = total


    returned = lax.all_to_all(item_grads, "tm", split_axis=0, concat_axis=0, tiled=True)
    shape = query_rows.shape
    grad_query, grad_key, grad_value = (g.reshape(shape) for g in unpack(returned))
    return (grad_query, grad_key, grad_value, grad_weight)


def solution(mesh):
    return jax.shard_map(
        local,
        mesh=mesh,
        in_specs=(
            P("tm", None, "track", None),
            P("tm", None, "track", None),
            P("tm", None, "track", None),
            P("tm", None, "track", None),
            P(None, "track"),
        ),
        out_specs=(
            P("tm", None, "track", None),
            P("tm", None, "track", None),
            P("tm", None, "track", None),
            P(("tm", "track"), None),
        ),
        check_vma=False,
    )
```
